32 devices in a mesh: expert: 16 (over z, x, core), tensor: 2 (over y).
Axes of the slice: x: 2, y: 2, z: 4, core: 2. Of those that a mesh axis runs over, the one named last changes fastest.
Arguments:
- hidden: bfloat16 [16, 128, 2048], P('expert'), may hold values from -6 to 6
- down_weight: bfloat16 [16, 2048, 7168], P('expert', None, 'tensor'), may hold values from -0.125 to 0.125
- expert_ids: int32 [256, 8], P('expert'), may hold values from 0 to 15, as said below
- gate_weights: float32 [256, 8], P('expert'), may hold values from 0.1 to 0.6
- residual: bfloat16 [256, 7168], P('expert', 'tensor'), may hold values from -36 to 36
- norm_gain: float32 [7168], replicated, may hold values from 0.1 to 1.9
- proj_weight: bfloat16 [7168, 2112], P(None, 'tensor'), may hold values from -0.0625 to 0.0625
Outputs:
- stream: bfloat16 [256, 7168], P('expert', 'tensor')
- latents: bfloat16 [256, 2112], P('expert', 'tensor')
The draws below stay inside these ranges and needn't reach their ends.
Inputs may be any that keep to these rules, and one draw needn't show every extreme that they name: `expert_ids`: experts 4 g to 4 g + 3 form node group g. Each token names 8 different experts, two in each of exactly 4 node groups. Within each aligned block of 16 tokens no expert is named by more than 8 tokens and no node group is used by more than 16 tokens; in every block some node group is used by exactly 16 tokens and each of its experts is named by exactly 8.
All inputs are finite; a program needn't handle non-finite values.
Results may differ from the reference program's by a relative error of at most 0.014.
Values may be sent and summed in bfloat16 or wider, within the bound.
No kernel may reach another device: no remote copies, remote signals or barrier semaphores. Data moves between devices by JAX's collectives and lax.ppermute only.
A program may use at most 64 MiB of HBM per device.

```python
import jax
import jax.numpy as jnp
from jax import lax

D = 7168
FF = 2048
TOPK = 8
NODE_SIZE = 4
GROUP_PICK = 4
EXPERTS = 16
NODE_GROUPS = 4
TOK_GRP = 16
TOKENS = 256
CAP = 8
GROUP_SLOTS = 128
LATENT = 2112
N_EXPERT = 16


def draw_residual(key, part):
    first_key, second_key = jax.random.split(jax.random.fold_in(key, 11))
    column_scale = 0.5 + jnp.arange(D, dtype=jnp.float32) / D
    values = jnp.clip(jax.random.normal(first_key, (TOKENS, D), jnp.float32), -6.0, 6.0)
    row_scale = jnp.exp(jax.random.uniform(second_key, (TOKENS, 1), jnp.float32, 0.0, 1.38))
    return (values * column_scale * row_scale).astype(jnp.bfloat16)


def permutations(key, count, length):
    keys = jax.random.split(key, count)
    return jax.vmap(lambda single: jax.random.permutation(single, length))(keys).astype(jnp.int32)


def draw_expert_ids(key, part):
    keys = jax.random.split(jax.random.fold_in(key, 23), 5)
    block_count = TOKENS // TOK_GRP
    group_count = EXPERTS // NODE_SIZE
    entry_count = GROUP_PICK * TOK_GRP
    top_load = 2 * CAP
    other_count = group_count - 1
    remainder = entry_count - top_load
    fill_base = remainder // other_count
    fill_extra = remainder % other_count
    spread_most = max(0, min(top_load - fill_base - 1, fill_base))
    pair_count = other_count // 2
    loads = jnp.broadcast_to(fill_base + (jnp.arange(other_count, dtype=jnp.int32) < fill_extra).astype(jnp.int32), (block_count, other_count))
    if pair_count > 0:
        moved = jax.random.randint(keys[0], (block_count, pair_count), 0, spread_most + 1).astype(jnp.int32)
        loads = loads.at[:, 0:2 * pair_count:2].add(moved)
        loads = loads.at[:, 1:2 * pair_count:2].add(-moved)
    loads = jnp.concatenate([jnp.full((block_count, 1), top_load, jnp.int32), loads], axis=1)
    group_order = permutations(keys[1], block_count, group_count)
    ends = jnp.cumsum(loads, axis=1)
    starts = ends - loads
    position = jnp.arange(entry_count, dtype=jnp.int32)
    rank_of = jnp.sum((ends[:, None, :] <= position[None, :, None]).astype(jnp.int32), axis=2)
    within = position[None, :] - jnp.take_along_axis(starts, rank_of, axis=1)
    group_of = jnp.take_along_axis(group_order, rank_of, axis=1)
    first_table = jnp.array([0, 2, 0, 1, 0, 1], jnp.int32)
    second_table = jnp.array([1, 3, 2, 3, 3, 2], jnp.int32)
    first_member = first_table[within % 6]
    second_member = second_table[within % 6]
    member_order = permutations(keys[2], block_count * group_count, NODE_SIZE).reshape(block_count, group_count * NODE_SIZE)
    first_expert = group_of * NODE_SIZE + jnp.take_along_axis(member_order, group_of * NODE_SIZE + first_member, axis=1)
    second_expert = group_of * NODE_SIZE + jnp.take_along_axis(member_order, group_of * NODE_SIZE + second_member, axis=1)
    chosen = jnp.stack([first_expert, second_expert], axis=2).reshape(block_count, GROUP_PICK, TOK_GRP, 2)
    chosen = jnp.transpose(chosen, (0, 2, 1, 3)).reshape(block_count, TOK_GRP, TOPK)
    token_order = permutations(keys[3], block_count, TOK_GRP)
    chosen = jnp.take_along_axis(chosen, token_order[:, :, None], axis=1)
    column_order = permutations(keys[4], block_count * TOK_GRP, TOPK).reshape(block_count, TOK_GRP, TOPK)
    chosen = jnp.take_along_axis(chosen, column_order, axis=2)
    return chosen.reshape(TOKENS, TOPK).astype(jnp.int32)


def levels(stream_key, extent, cuts, low, largest):
    def one(dim, shards_of):
        draws = jax.random.uniform(jax.random.fold_in(jax.random.fold_in(stream_key, 6), dim), (shards_of,), jnp.float32, low / len(cuts), largest / len(cuts))
        return jnp.repeat(jnp.exp(draws), extent[dim] // shards_of).reshape((-1,) + (1,) * (len(extent) - dim - 1))

    loudness = one(*cuts[0])
    for cut in cuts[1:]:
        loudness = loudness * one(*cut)
    return loudness


def normal_values(rng, extent, scale, reach, cuts=(), held_as=jnp.bfloat16):
    level = levels(rng, extent, cuts, -0.22, 0.18) if cuts else 1.0
    values = jax.random.normal(rng, extent, jnp.float32) * scale * level
    return jnp.minimum(jnp.maximum(values, -reach), reach).astype(held_as)


def setup_inputs(seed: int = 0) -> dict:
    seeds = jax.random.split(jax.random.key(seed), 8)
    hidden = normal_values(seeds[0], (EXPERTS, GROUP_SLOTS, FF), 1.0, 6.0, ((0, 16),))
    down_weight = normal_values(seeds[1], (EXPERTS, FF, D), FF ** -0.5, 0.125, ((0, 16), (2, 2)))
    expert_ids = draw_expert_ids(jax.random.fold_in(seeds[7], 71), 0)
    gate_weights = jnp.clip(0.1 + 0.5 * jax.random.uniform(seeds[3], (TOKENS, TOPK), jnp.float32) ** levels(seeds[3], (TOKENS, TOPK), ((0, 16),), -0.2, 0.2), 0.1, 0.6)
    residual = draw_residual(jax.random.fold_in(seeds[7], 71), 0)
    norm_gain = jnp.clip(1.0 + 0.18 * jax.random.normal(seeds[5], (D,), jnp.float32), 0.1, 1.9)
    proj_weight = normal_values(seeds[6], (D, LATENT), D ** -0.5, 0.0625, ((1, 2),))
    return {"hidden": hidden, "down_weight": down_weight, "expert_ids": expert_ids, "gate_weights": gate_weights, "residual": residual, "norm_gain": norm_gain, "proj_weight": proj_weight}


epsilon = 1e-06

def reference(hidden, down_weight, expert_ids, gate_weights, residual, norm_gain, proj_weight):
    groups = expert_ids.reshape(N_EXPERT, TOK_GRP, TOPK)
    expert_range = jnp.arange(EXPERTS, dtype=jnp.int32)
    counts = lax.optimization_barrier(jnp.sum((groups[:, :, :, None] == expert_range).astype(jnp.int32), axis=2))
    before = jnp.cumsum(counts, axis=1) - counts
    slots = jnp.take_along_axis(before, groups, axis=2).reshape(TOKENS, TOPK).astype(jnp.int32)
    owner_base = jnp.arange(TOKENS, dtype=jnp.int32) // TOK_GRP * CAP
    slot_rows = (owner_base[:, None] + slots).astype(jnp.int32)

    def add_group(summed, group):

        def add_expert(partial_value, member):
            expert = (group * NODE_SIZE + member).astype(jnp.int32)
            product = jnp.dot(hidden[expert], down_weight[expert], preferred_element_type=jnp.float32).astype(jnp.bfloat16)
            chosen = expert_ids == expert
            weighting = lax.optimization_barrier(jnp.sum(jnp.where(chosen, gate_weights, jnp.zeros_like(gate_weights)), axis=1))
            row_index = lax.optimization_barrier(jnp.sum(jnp.where(chosen, slot_rows, jnp.zeros_like(slot_rows)), axis=1)).astype(jnp.int32)
            addition = weighting[:, None] * product[row_index].astype(jnp.float32)
            return (partial_value + addition, None)
        partial_value, _ = lax.scan(add_expert, jnp.zeros((TOKENS, D), jnp.float32), jnp.arange(NODE_SIZE, dtype=jnp.int32))
        rounded = lax.optimization_barrier(partial_value.astype(jnp.bfloat16))
        return (summed + rounded.astype(jnp.float32), None)
    summed, _ = lax.scan(add_group, residual.astype(jnp.float32), jnp.arange(NODE_GROUPS, dtype=jnp.int32))
    stream = summed.astype(jnp.bfloat16)
    stream_wide = stream.astype(jnp.float32)
    energy = lax.optimization_barrier(jnp.mean(stream_wide * stream_wide, axis=1))
    normed = (stream_wide * norm_gain).astype(jnp.bfloat16)
    projected = jnp.dot(normed, proj_weight, preferred_element_type=jnp.float32)
    latents = (projected * lax.rsqrt(energy + epsilon)[:, None]).astype(jnp.bfloat16)
    return (stream, latents)
```

```python
import functools

import jax
import jax.numpy as jnp
from jax import lax
from jax.experimental import pallas as pl
from jax.experimental.pallas import tpu as pltpu
from jax.sharding import PartitionSpec as P

NODE_SIZE = 4
LANES = 128
MIB = 1 << 20


epsilon = 1e-06

VMEM = pl.BlockSpec(memory_space=pltpu.VMEM)
SMEM = pl.BlockSpec(memory_space=pltpu.SMEM)
ANY = pl.BlockSpec(memory_space=pl.ANY)
HBM = pl.BlockSpec(memory_space=pltpu.HBM)


def shape_of(shape, dtype):
    return jax.ShapeDtypeStruct(shape, dtype)


def cut(columns):
    tiles = columns // LANES
    if columns % LANES or tiles < 8:
        return [(0, columns)]
    first = tiles // 2 * LANES
    return [(0, first), (first, columns - first)]


def block_width(width):
    for tiles in (2, 3, 1):
        if width % (tiles * LANES) == 0:
            return tiles * LANES
    return width


def routing(index, experts, capacity, ids, gates):
    groups = experts // NODE_SIZE
    slots = experts * capacity
    tokens = ids.shape[1]
    row = lax.broadcasted_iota(jnp.int32, (slots, tokens), 0)
    slot = row % capacity
    group = row // capacity % groups
    member = row // (capacity * groups)
    expert = index ^ (group * NODE_SIZE + member)
    named = jnp.zeros((slots, tokens), jnp.float32)
    gate = jnp.zeros((slots, tokens), jnp.float32)
    for k in range(ids.shape[0]):
        hit = ids[k : k + 1, :] == expert
        named = named + jnp.where(hit, 1.0, 0.0)
        gate = gate + jnp.where(hit, gates[k : k + 1, :], 0.0)
    earlier = lax.broadcasted_iota(jnp.int32, (tokens, tokens), 0) < lax.broadcasted_iota(
        jnp.int32, (tokens, tokens), 1
    )
    before = jnp.dot(named, jnp.where(earlier, 1.0, 0.0), preferred_element_type=jnp.float32)
    full = jnp.where(before == slot.astype(jnp.float32), gate, 0.0)
    return [jnp.where(group == d, full, 0.0).T for d in range(groups)]


def down_kernel(experts, first, width, block, with_routing, *refs):
    if with_routing:
        index_ref, hidden_ref, weight_ref, ids_ref, gates_ref = refs[:5]
        rest = refs[5:]
    else:
        index_ref, hidden_ref, weight_ref = refs[:3]
        rest = refs[3:]
    out_refs, rest = rest[:NODE_SIZE], rest[NODE_SIZE:]
    groups = experts // NODE_SIZE
    if with_routing:
        gate_refs, rest = rest[:groups], rest[groups:]
    weights, wide, ordered, sems = rest
    index = index_ref[0]
    blocks = width // block
    copies = [
        pltpu.make_async_copy(
            weight_ref.at[0, :, pl.ds(first + i * block, block)], weights.at[i], sems.at[i]
        )
        for i in range(blocks)
    ]
    for copy in copies:
        copy.start()
    rows = wide.shape[0]
    capacity = rows // experts
    wide[...] = hidden_ref[0].astype(jnp.float32)
    for j in range(NODE_SIZE):
        for d in range(0, groups, 2):
            pair = []
            for other in (d, d + 1):
                owner = index ^ (other * NODE_SIZE + j)
                pair.append(wide[pl.ds(pl.multiple_of(owner * capacity, capacity), capacity), :])
            start = (j * groups + d) * capacity
            ordered[start : start + 2 * capacity, :] = jnp.concatenate(pair, axis=0).astype(
                jnp.bfloat16
            )
    if with_routing:
        parts = routing(index, experts, capacity, ids_ref[...], gates_ref[...])
        for ref, part in zip(gate_refs, parts):
            ref[...] = part
    share = rows // NODE_SIZE
    for i, copy in enumerate(copies):
        copy.wait()
        product = jnp.dot(
            ordered[...], weights[i], preferred_element_type=jnp.float32
        ).astype(jnp.bfloat16)
        for j in range(NODE_SIZE):
            out_refs[j][:, i * block : (i + 1) * block] = product[j * share : (j + 1) * share, :]


def down(index, hidden, down_weight, first, width, experts, ids=None, gates=None):
    block = block_width(width)
    rows, depth = hidden.shape[1:]
    share = rows // NODE_SIZE
    groups = experts // NODE_SIZE
    out_shape = [shape_of((share, width), jnp.bfloat16)] * NODE_SIZE
    in_specs = [SMEM, VMEM, HBM]
    args = [index, hidden, down_weight]
    if ids is not None:
        out_shape += [shape_of((ids.shape[1], rows), jnp.float32)] * groups
        in_specs += [VMEM, VMEM]
        args += [ids, gates]
    return pl.pallas_call(
        functools.partial(down_kernel, experts, first, width, block, ids is not None),
        out_shape=out_shape,
        in_specs=in_specs,
        out_specs=[VMEM] * len(out_shape),
        scratch_shapes=[
            pltpu.VMEM((width // block, depth, block), jnp.bfloat16),
            pltpu.VMEM((rows, depth), jnp.float32),
            pltpu.VMEM((rows, depth), jnp.bfloat16),
            pltpu.SemaphoreType.DMA((width // block,)),
        ],
        name="down",
        compiler_params=pltpu.CompilerParams(vmem_limit_bytes=48 * MIB if rows > 512 else 24 * MIB),
    )(*args)


def combine_kernel(groups, *refs):
    gate_refs = refs[:groups]
    row_refs = refs[groups : groups + NODE_SIZE]
    out_refs = refs[groups + NODE_SIZE :]
    tokens = gate_refs[0].shape[0]
    rows = jnp.concatenate([ref[...] for ref in row_refs], axis=0)
    together = groups if groups * tokens <= LANES else 1
    for base in range(0, groups, together):
        gate = jnp.concatenate([ref[...] for ref in gate_refs[base : base + together]], axis=0)
        high = gate.astype(jnp.bfloat16)
        low = (gate - high.astype(jnp.float32)).astype(jnp.bfloat16)
        both = jnp.dot(
            jnp.concatenate([high, low], axis=0), rows, preferred_element_type=jnp.float32
        )
        half = together * tokens
        part = (both[:half] + both[half:]).astype(jnp.bfloat16)
        for d in range(together):
            out_refs[base + d][...] = part[d * tokens : (d + 1) * tokens]


def combine(gates, rows):
    groups = len(gates)
    tokens = gates[0].shape[0]
    width = rows[0].shape[1]
    return pl.pallas_call(
        functools.partial(combine_kernel, groups),
        out_shape=[shape_of((tokens, width), jnp.bfloat16)] * groups,
        in_specs=[VMEM] * (groups + NODE_SIZE),
        out_specs=[VMEM] * groups,
        name="combine",
        compiler_params=pltpu.CompilerParams(vmem_limit_bytes=(40 if tokens > 16 else 8) * MIB),
    )(*gates, *rows)


def project_kernel(spans, columns, final, *refs):
    base_ref, gain_ref, weight_ref, refs = refs[0], refs[1], refs[2], refs[3:]
    section_refs, refs = refs[: len(spans)], refs[len(spans) :]
    carried = len(refs) - (1 if final else 2) == 2
    total = energy = None
    if carried:
        total, energy = refs[0][...], refs[1][...]
        refs = refs[2:]
    for n, (first, width) in enumerate(spans):
        start = pl.multiple_of(base_ref[n] * columns + first, LANES)
        wide = section_refs[n][...].astype(jnp.float32)
        square = jnp.sum(wide * wide, axis=1, keepdims=True)
        normed = (wide * gain_ref[:, pl.ds(start, width)]).astype(jnp.bfloat16)
        product = lax.dot_general(
            normed,
            weight_ref[:, pl.ds(start, width)],
            (((1,), (1,)), ((), ())),
            preferred_element_type=jnp.float32,
        )
        total = product if total is None else total + product
        energy = square if energy is None else energy + square
    if final:
        scale = lax.rsqrt(energy / final + epsilon)
        refs[0][...] = (total * scale).astype(jnp.bfloat16)
    else:
        refs[0][...] = total
        refs[1][...] = energy


def project(bases, gain, weight, sections, spans, columns, carried=(), final=0):
    tokens = sections[0].shape[0]
    latents = weight.shape[0]
    if final:
        out_shape = [shape_of((tokens, latents), jnp.bfloat16)]
    else:
        out_shape = [shape_of((tokens, latents), jnp.float32), shape_of((tokens, 1), jnp.float32)]
    return pl.pallas_call(
        functools.partial(project_kernel, spans, columns, final),
        out_shape=out_shape,
        in_specs=[SMEM] + [VMEM] * (2 + len(sections) + len(carried)),
        out_specs=[VMEM] * len(out_shape),
        name="project",
        compiler_params=pltpu.CompilerParams(vmem_limit_bytes=8 * MIB),
    )(bases, gain, weight, *sections, *carried)


def on_device(hidden, down_weight, expert_ids, gate_weights, residual, norm_gain, proj_weight):
    experts = lax.axis_size("expert")
    tensors = lax.axis_size("tensor")
    groups = experts // NODE_SIZE
    columns = down_weight.shape[2]
    index = lax.axis_index("expert").astype(jnp.int32)
    column_index = lax.axis_index("tensor").astype(jnp.int32)

    def swap(value, bits):
        return lax.ppermute(value, "expert", [(i, i ^ bits) for i in range(experts)])

    def swap_columns(value, bits):
        return lax.ppermute(value, "tensor", [(i, i ^ bits) for i in range(tensors)])

    spans = cut(columns)
    ids, gates = expert_ids.T, gate_weights.T
    place = index.reshape(1)
    arrived = []
    routed = None
    for first, width in spans:
        if routed is None:
            results = down(place, hidden, down_weight, first, width, experts, ids, gates)
            rows, own_routed = results[:NODE_SIZE], results[NODE_SIZE:]
        else:
            rows = down(place, hidden, down_weight, first, width, experts)
        arrived.append([rows[0]] + [swap(rows[j], j) for j in range(1, NODE_SIZE)])
        if routed is None:
            routed = [own_routed[0]] + [
                swap(own_routed[d], d * NODE_SIZE) for d in range(1, groups)
            ]
    streams = []
    for (first, width), rows in zip(spans, arrived):
        parts = combine(routed, rows)
        received = [parts[0]] + [swap(parts[d], d * NODE_SIZE) for d in range(1, groups)]
        summed = residual[:, first : first + width].astype(jnp.float32)
        for part in received:
            summed = summed + part.astype(jnp.float32)
        streams.append(summed.astype(jnp.bfloat16))
    stream = jnp.concatenate(streams, axis=1) if len(streams) > 1 else streams[0]
    features = columns * tensors
    if columns % LANES or len(spans) < 2 or tensors != 2:
        wide = lax.all_gather(stream, "tensor", axis=1, tiled=True).astype(jnp.float32)
        normed = (wide * norm_gain).astype(jnp.bfloat16)
        added = jnp.dot(normed, proj_weight, preferred_element_type=jnp.float32)
        energy = jnp.sum(wide * wide, axis=1)
        inverse = lax.rsqrt(energy / features + epsilon)
        return (stream, (added * inverse[:, None]).astype(jnp.bfloat16))
    others = [swap_columns(section, 1) for section in streams]
    gain = norm_gain.reshape(1, features)
    weight = proj_weight.T
    near, far = column_index, column_index ^ 1
    carried = project(near.reshape(1), gain, weight, streams[:1], spans[:1], columns)
    for n in range(1, len(spans)):
        carried = project(
            jnp.stack([near, far]),
            gain,
            weight,
            [streams[n], others[n - 1]],
            [spans[n], spans[n - 1]],
            columns,
            carried,
        )
    (latents,) = project(
        far.reshape(1), gain, weight, others[-1:], spans[-1:], columns, carried, features
    )
    return (stream, latents)


def solution(mesh):
    return jax.shard_map(
        on_device,
        mesh=mesh,
        in_specs=(
            P("expert", None, None),
            P("expert", None, "tensor"),
            P("expert", None),
            P("expert", None),
            P("expert", "tensor"),
            P(),
            P(None, "tensor"),
        ),
        out_specs=(P("expert", "tensor"), P("expert", "tensor")),
        check_vma=False,
    )
```

```python
import functools

import jax
import jax.numpy as jnp
from jax import lax
from jax.experimental import pallas as pl
from jax.experimental.pallas import tpu as pltpu
from jax.sharding import PartitionSpec as P

NODE_SIZE = 4
LANES = 128
MIB = 1 << 20
ADD_COST = 64 * MIB


epsilon = 1e-06

VMEM = pl.BlockSpec(memory_space=pltpu.VMEM)
SMEM = pl.BlockSpec(memory_space=pltpu.SMEM)
ANY = pl.BlockSpec(memory_space=pl.ANY)
HBM = pl.BlockSpec(memory_space=pltpu.HBM)


def shape_of(shape, dtype):
    return jax.ShapeDtypeStruct(shape, dtype)


def block_width(width):
    for tiles in (4, 2, 3, 1):
        if width % (tiles * LANES) == 0:
            return tiles * LANES
    return width


def halves(groups):
    if groups < 4 or groups % 4:
        return [(0, groups)]
    return [(groups // 2, groups // 2), (0, groups // 2)]


def pieces_of(spans):
    outputs = [[(j, low, count) for low, count in spans] for j in (0, 1)]
    low, count = spans[0]
    outputs.append([(2, low, count), (3, low, count)])
    for low, count in spans[1:]:
        outputs += [[(2, low, count)], [(3, low, count)]]
    return outputs


def down_kernel(experts, outputs, block, hidden_hbm, weight_hbm, *refs):
    out_refs = refs[: len(outputs)]
    hidden, wide, ordered, weights, hidden_sem, weight_sems = refs[len(outputs) :]
    index = lax.axis_index("expert")
    first_copy = pltpu.make_async_copy(hidden_hbm.at[0], hidden, hidden_sem)
    copies = [
        pltpu.make_async_copy(
            weight_hbm.at[0, :, pl.ds(i * block, block)], weights.at[i], weight_sems.at[i]
        )
        for i in range(weights.shape[0])
    ]
    first_copy.start()
    for copy in copies:
        copy.start()
    rows = hidden.shape[0]
    capacity = rows // experts
    first_copy.wait()
    wide[...] = hidden[...].astype(jnp.float32)
    start = 0
    starts = []
    for pieces in outputs:
        starts.append(start)
        for j, low, count in pieces:
            for d in range(low, low + count, 2):
                pair = []
                for other in (d, d + 1):
                    owner = index ^ (other * NODE_SIZE + j)
                    pair.append(
                        wide[pl.ds(pl.multiple_of(owner * capacity, capacity), capacity), :]
                    )
                ordered[start : start + 2 * capacity, :] = jnp.concatenate(pair, axis=0).astype(
                    jnp.bfloat16
                )
                start += 2 * capacity
    starts.append(start)
    for i, copy in enumerate(copies):
        copy.wait()
        product = jnp.dot(
            ordered[...], weights[i], preferred_element_type=jnp.float32
        ).astype(jnp.bfloat16)
        for ref, begin, end in zip(out_refs, starts[:-1], starts[1:]):
            ref[:, i * block : (i + 1) * block] = product[begin:end, :]


def down(hidden, down_weight, experts, spans):
    rows, depth = hidden.shape[1:]
    columns = down_weight.shape[2]
    capacity = rows // experts
    block = block_width(columns)
    outputs = pieces_of(spans)
    out_shape = [
        shape_of((sum(count for _, _, count in pieces) * capacity, columns), jnp.bfloat16)
        for pieces in outputs
    ]
    return pl.pallas_call(
        functools.partial(down_kernel, experts, outputs, block),
        out_shape=out_shape,
        in_specs=[ANY, ANY],
        out_specs=[VMEM] * len(out_shape),
        scratch_shapes=[
            pltpu.VMEM((rows, depth), jnp.bfloat16),
            pltpu.VMEM((rows, depth), jnp.float32),
            pltpu.VMEM((rows, depth), jnp.bfloat16),
            pltpu.VMEM((columns // block, depth, block), jnp.bfloat16),
            pltpu.SemaphoreType.DMA(()),
            pltpu.SemaphoreType.DMA((columns // block,)),
        ],
        name="down",
        cost_estimate=pl.CostEstimate(
            flops=2 * rows * depth * columns, bytes_accessed=2 * depth * columns, transcendentals=0
        ),
        compiler_params=pltpu.CompilerParams(vmem_limit_bytes=50 * MIB),
    )(hidden, down_weight)


def gates_of(index, low, count, capacity, tokens, chosen):
    shape = (NODE_SIZE * count * capacity, tokens)
    row = lax.broadcasted_iota(jnp.int32, shape, 0)
    slot = (row % capacity).astype(jnp.float32)
    group = row // capacity % count + low
    expert = (index ^ (row // (capacity * count))).astype(jnp.float32)
    earlier = lax.broadcasted_iota(jnp.int32, (tokens, tokens), 0) < lax.broadcasted_iota(
        jnp.int32, (tokens, tokens), 1
    )
    earlier = jnp.where(earlier, 1.0, 0.0)
    found = []
    for d in range(low, low + count):
        picks = chosen[d - low].shape[0] // 2
        ids, gates = chosen[d - low][:picks], chosen[d - low][picks:]
        named = jnp.zeros(shape, jnp.float32)
        gate = jnp.zeros(shape, jnp.float32)
        for k in range(picks):
            hit = ids[k : k + 1, :] == expert
            named = named + jnp.where(hit, 1.0, 0.0)
            gate = gate + jnp.where(hit, gates[k : k + 1, :], 0.0)
        before = jnp.dot(named, earlier, preferred_element_type=jnp.float32)
        found.append(jnp.where((before == slot) & (group == d), gate, 0.0).T)
    return found


def combine_kernel(low, count, capacity, begins, *refs):
    chosen_refs = refs[:count]
    row_refs = refs[count : count + NODE_SIZE]
    out_refs = refs[len(refs) - count :]
    tokens = chosen_refs[0].shape[1]
    index = lax.axis_index("expert")
    found = gates_of(index, low, count, capacity, tokens, [ref[...] for ref in chosen_refs])
    rows = jnp.concatenate(
        [ref[begin : begin + count * capacity] for ref, begin in zip(row_refs, begins)], axis=0
    )
    together = count if count * tokens <= LANES else 1
    for base in range(0, count, together):
        gate = jnp.concatenate(found[base : base + together], axis=0)
        high = gate.astype(jnp.bfloat16)
        rest = (gate - high.astype(jnp.float32)).astype(jnp.bfloat16)
        both = jnp.dot(
            jnp.concatenate([high, rest], axis=0), rows, preferred_element_type=jnp.float32
        )
        half = together * tokens
        part = (both[:half] + both[half:]).astype(jnp.bfloat16)
        for d in range(together):
            out_refs[base + d][...] = part[d * tokens : (d + 1) * tokens]


def combine(chosen, rows, begins, low, capacity, after):
    count = len(chosen)
    tokens = chosen[0].shape[1]
    columns = rows[0].shape[1]
    return pl.pallas_call(
        functools.partial(combine_kernel, low, count, capacity, begins),
        out_shape=[shape_of((tokens, columns), jnp.bfloat16)] * count,
        in_specs=[VMEM] * (count + NODE_SIZE) + [ANY] * len(after),
        out_specs=[VMEM] * count,
        name="combine",
        cost_estimate=pl.CostEstimate(
            flops=4 * count * tokens * LANES * columns,
            bytes_accessed=4 * count * tokens * columns,
            transcendentals=0,
        ),
        compiler_params=pltpu.CompilerParams(vmem_limit_bytes=(40 if tokens > 16 else 8) * MIB),
    )(*chosen, *rows, *after)


def add_kernel(base_ref, *refs):
    total = base_ref[...].astype(jnp.float32)
    for ref in refs[:-1]:
        total = total + ref[...].astype(jnp.float32)
    refs[-1][...] = total


def add(base, parts):
    return pl.pallas_call(
        add_kernel,
        out_shape=shape_of(base.shape, jnp.float32),
        in_specs=[VMEM] * (1 + len(parts)),
        out_specs=VMEM,
        name="add",
        cost_estimate=pl.CostEstimate(
            flops=0, bytes_accessed=ADD_COST, transcendentals=0
        ),
        compiler_params=pltpu.CompilerParams(vmem_limit_bytes=(40 if base.shape[0] > 16 else 8) * MIB),
    )(base, *parts)


def fetch_kernel(columns, flip, pieces, source_hbm, after_ref, out_ref, sems):
    width = columns // pieces
    base = (lax.axis_index("tensor") ^ flip) * columns
    copies = [
        pltpu.make_async_copy(
            source_hbm.at[:, pl.ds(pl.multiple_of(base + i * width, LANES), width)],
            out_ref.at[:, pl.ds(i * width, width)],
            sems.at[i],
        )
        for i in range(pieces)
    ]
    for copy in copies:
        copy.start()
    for copy in copies:
        copy.wait()


def fetch(source, columns, flip, after):
    pieces = 4 if columns // 4 % LANES == 0 else 1
    return pl.pallas_call(
        functools.partial(fetch_kernel, columns, flip, pieces),
        out_shape=pltpu.VMEM((source.shape[0], columns), source.dtype),
        in_specs=[ANY, ANY],
        out_specs=VMEM,
        scratch_shapes=[pltpu.SemaphoreType.DMA((pieces,))],
        name="fetch",
        cost_estimate=pl.CostEstimate(
            flops=0, bytes_accessed=2 * source.shape[0] * columns, transcendentals=0
        ),
        compiler_params=pltpu.CompilerParams(vmem_limit_bytes=40 * MIB),
    )(source, after)


def project_kernel(block, features, *refs):
    gain_ref, weight_ref, section_ref = refs[:3]
    refs = refs[3:]
    columns = section_ref.shape[1]
    base = lax.axis_index("tensor")
    total = energy = None
    if features:
        base = base ^ 1
        total, energy = refs[0][...], refs[1][...]
    for i in range(0, columns, block):
        wide = section_ref[:, i : i + block].astype(jnp.float32)
        square = jnp.sum(wide * wide, axis=1, keepdims=True)
        begin = pl.multiple_of(base * columns + i, LANES)
        normed = (wide * gain_ref[:, pl.ds(begin, block)]).astype(jnp.bfloat16)
        product = lax.dot_general(
            normed,
            weight_ref[:, i : i + block],
            (((1,), (1,)), ((), ())),
            preferred_element_type=jnp.float32,
        )
        total = product if total is None else total + product
        energy = square if energy is None else energy + square
    if features:
        scale = lax.rsqrt(energy / features + epsilon)
        refs[2][...] = (total * scale).astype(jnp.bfloat16)
    else:
        refs[0][...] = total
        refs[1][...] = energy


def project(gain, weight, section, carried=(), features=0):
    tokens, columns = section.shape
    latents = weight.shape[0]
    block = columns // 4 if columns // 4 % LANES == 0 else columns
    if features:
        out_shape = [shape_of((tokens, latents), jnp.bfloat16)]
    else:
        out_shape = [shape_of((tokens, latents), jnp.float32), shape_of((tokens, 1), jnp.float32)]
    return pl.pallas_call(
        functools.partial(project_kernel, block, features),
        out_shape=out_shape,
        in_specs=[VMEM] * (3 + len(carried)),
        out_specs=[VMEM] * len(out_shape),
        name="project",
        cost_estimate=pl.CostEstimate(
            flops=64 * tokens * latents * columns, bytes_accessed=0, transcendentals=0
        ),
        compiler_params=pltpu.CompilerParams(vmem_limit_bytes=8 * MIB),
    )(gain, weight, section, *carried)


def on_device(hidden, down_weight, expert_ids, gate_weights, residual, norm_gain, proj_weight):
    experts = lax.axis_size("expert")
    tensors = lax.axis_size("tensor")
    groups = experts // NODE_SIZE
    columns = down_weight.shape[2]
    capacity = hidden.shape[1] // experts
    features = columns * tensors
    spans = halves(groups)

    def swap(value, bits):
        return lax.ppermute(value, "expert", [(i, i ^ bits) for i in range(experts)])

    results = down(hidden, down_weight, experts, spans)
    results, expert_ids, gate_weights = lax.optimization_barrier(
        (results, expert_ids, gate_weights)
    )
    own, near, first, *rest = results
    first = swap(first, 2)
    near = swap(near, 1)
    rest = [swap(rows, 2 + n % 2) for n, rows in enumerate(rest)]
    chosen = [jnp.concatenate([expert_ids.T.astype(jnp.float32), gate_weights.T], axis=0)]
    while len(chosen) < groups:
        sent = jnp.concatenate(chosen, axis=0)
        got = swap(sent, len(chosen) * NODE_SIZE)
        chosen += jnp.split(got, len(chosen), axis=0)
    weight = proj_weight.T
    summed = residual
    begin = 0
    after = ()
    paired = columns % LANES == 0 and tensors == 2 and len(spans) == 2
    for n, (low, count) in enumerate(spans):
        height = count * capacity
        if n:
            far = rest[2 * n - 2 : 2 * n]
        else:
            far = [first, swap(first[height:], 1)]
        parts = combine(
            chosen[low : low + count],
            [own, near, *far],
            [begin, begin, 0, 0],
            low,
            capacity,
            after,
        )
        begin += height
        after = parts[:1]
        moved = [swap(part, d * NODE_SIZE) if d else part for d, part in enumerate(parts, low)]
        if low:
            summed = add(summed, moved)
        else:
            for part in moved:
                summed = summed.astype(jnp.float32) + part.astype(jnp.float32)
    stream = summed.astype(jnp.bfloat16)
    if not paired:
        wide = lax.all_gather(stream, "tensor", axis=1, tiled=True).astype(jnp.float32)
        normed = (wide * norm_gain).astype(jnp.bfloat16)
        added = jnp.dot(normed, proj_weight, preferred_element_type=jnp.float32)
        energy = jnp.sum(wide * wide, axis=1)
        inverse = lax.rsqrt(energy / features + epsilon)
        return (stream, (added * inverse[:, None]).astype(jnp.bfloat16))
    held = [fetch(weight, columns, flip, *after) for flip in range(2)]
    stream, held = lax.optimization_barrier((stream, held))
    other = lax.ppermute(stream, "tensor", [(i, i ^ 1) for i in range(tensors)])
    gain = norm_gain.reshape(1, features)
    carried = project(gain, held[0], stream)
    (latents,) = project(gain, held[1], other, carried, features)
    return (stream, latents)


def solution(mesh):
    return jax.shard_map(
        on_device,
        mesh=mesh,
        in_specs=(
            P("expert", None, None),
            P("expert", None, "tensor"),
            P("expert", None),
            P("expert", None),
            P("expert", "tensor"),
            P(),
            P(None, "tensor"),
        ),
        out_specs=(P("expert", "tensor"), P("expert", "tensor")),
        check_vma=False,
    )
```

```python
import functools

import jax
import jax.numpy as jnp
from jax import lax
from jax.experimental import pallas as pl
from jax.experimental.pallas import tpu as pltpu
from jax.sharding import PartitionSpec as P

NODE_SIZE = 4
LANES = 128
MIB = 1 << 20
AHEAD = 3
DEPTH_STEPS = 8
ADD_COST = 64 * MIB


epsilon = 1e-06

VMEM = pl.BlockSpec(memory_space=pltpu.VMEM)
SMEM = pl.BlockSpec(memory_space=pltpu.SMEM)
ANY = pl.BlockSpec(memory_space=pl.ANY)
HBM = pl.BlockSpec(memory_space=pltpu.HBM)


def shape_of(shape, dtype):
    return jax.ShapeDtypeStruct(shape, dtype)


def block_width(width):
    for tiles in (4, 2, 3, 1):
        if width % (tiles * LANES) == 0:
            return tiles * LANES
    return width


def halves(groups):
    if groups < 4 or groups % 4:
        return [(0, groups)]
    return [(groups // 2, groups // 2), (0, groups // 2)]


def pieces_of(spans):
    outputs = [[(j, low, count) for low, count in spans] for j in (0, 1)]
    low, count = spans[0]
    outputs.append([(2, low, count), (3, low, count)])
    for low, count in spans[1:]:
        outputs += [[(2, low, count)], [(3, low, count)]]
    return outputs


def down_kernel(experts, outputs, hidden_hbm, weight_hbm, *refs):
    out_refs = refs[: len(outputs)]
    hidden, wide, ordered, weights, total, hidden_sem, weight_sems = refs[len(outputs) :]
    index = lax.axis_index("expert")
    steps, depth = weights.shape[:2]
    first_copy = pltpu.make_async_copy(hidden_hbm.at[0], hidden, hidden_sem)
    copies = [
        pltpu.make_async_copy(
            weight_hbm.at[0, pl.ds(i * depth, depth)], weights.at[i], weight_sems.at[i]
        )
        for i in range(steps)
    ]
    first_copy.start()
    for copy in copies[:AHEAD]:
        copy.start()
    rows = hidden.shape[0]
    capacity = rows // experts
    first_copy.wait()
    wide[...] = hidden[...].astype(jnp.float32)
    start = 0
    starts = []
    for pieces in outputs:
        starts.append(start)
        for j, low, count in pieces:
            for d in range(low, low + count, 2):
                pair = []
                for other in (d, d + 1):
                    owner = index ^ (other * NODE_SIZE + j)
                    pair.append(
                        wide[pl.ds(pl.multiple_of(owner * capacity, capacity), capacity), :]
                    )
                ordered[start : start + 2 * capacity, :] = jnp.concatenate(pair, axis=0).astype(
                    jnp.bfloat16
                )
                start += 2 * capacity
    starts.append(start)
    columns = total.shape[1]
    block = block_width(columns)
    for i, copy in enumerate(copies):
        copy.wait()
        if i + AHEAD < steps:
            copies[i + AHEAD].start()
        for first in range(0, columns, block):
            product = jnp.dot(
                ordered[:, i * depth : (i + 1) * depth],
                weights[i, :, first : first + block],
                preferred_element_type=jnp.float32,
            )
            if i:
                product = total[:, first : first + block] + product
            if i < steps - 1:
                total[:, first : first + block] = product
            else:
                rounded = product.astype(jnp.bfloat16)
                for ref, begin, end in zip(out_refs, starts[:-1], starts[1:]):
                    ref[:, first : first + block] = rounded[begin:end, :]


def down(hidden, down_weight, experts, spans):
    rows, depth = hidden.shape[1:]
    columns = down_weight.shape[2]
    capacity = rows // experts
    outputs = pieces_of(spans)
    out_shape = [
        shape_of((sum(count for _, _, count in pieces) * capacity, columns), jnp.bfloat16)
        for pieces in outputs
    ]
    return pl.pallas_call(
        functools.partial(down_kernel, experts, outputs),
        out_shape=out_shape,
        in_specs=[ANY, ANY],
        out_specs=[VMEM] * len(out_shape),
        scratch_shapes=[
            pltpu.VMEM((rows, depth), jnp.bfloat16),
            pltpu.VMEM((rows, depth), jnp.float32),
            pltpu.VMEM((rows, depth), jnp.bfloat16),
            pltpu.VMEM((DEPTH_STEPS, depth // DEPTH_STEPS, columns), jnp.bfloat16),
            pltpu.VMEM((rows, columns), jnp.float32),
            pltpu.SemaphoreType.DMA(()),
            pltpu.SemaphoreType.DMA((DEPTH_STEPS,)),
        ],
        name="down",
        cost_estimate=pl.CostEstimate(
            flops=2 * rows * depth * columns, bytes_accessed=2 * depth * columns, transcendentals=0
        ),
        compiler_params=pltpu.CompilerParams(vmem_limit_bytes=53 * MIB),
    )(hidden, down_weight)


def gates_of(index, low, count, capacity, tokens, chosen):
    shape = (NODE_SIZE * count * capacity, tokens)
    row = lax.broadcasted_iota(jnp.int32, shape, 0)
    slot = (row % capacity).astype(jnp.float32)
    group = row // capacity % count + low
    expert = (index ^ (row // (capacity * count))).astype(jnp.float32)
    earlier = lax.broadcasted_iota(jnp.int32, (tokens, tokens), 0) < lax.broadcasted_iota(
        jnp.int32, (tokens, tokens), 1
    )
    earlier = jnp.where(earlier, 1.0, 0.0)
    found = []
    for d in range(low, low + count):
        picks = chosen[d - low].shape[0] // 2
        ids, gates = chosen[d - low][:picks], chosen[d - low][picks:]
        named = jnp.zeros(shape, jnp.float32)
        gate = jnp.zeros(shape, jnp.float32)
        for k in range(picks):
            hit = ids[k : k + 1, :] == expert
            named = named + jnp.where(hit, 1.0, 0.0)
            gate = gate + jnp.where(hit, gates[k : k + 1, :], 0.0)
        before = jnp.dot(named, earlier, preferred_element_type=jnp.float32)
        found.append(jnp.where((before == slot) & (group == d), gate, 0.0).T)
    return found


def combine_kernel(low, count, capacity, begins, *refs):
    chosen_refs = refs[:count]
    row_refs = refs[count : count + NODE_SIZE]
    out_refs = refs[len(refs) - count :]
    tokens = chosen_refs[0].shape[1]
    index = lax.axis_index("expert")
    found = gates_of(index, low, count, capacity, tokens, [ref[...] for ref in chosen_refs])
    rows = jnp.concatenate(
        [ref[begin : begin + count * capacity] for ref, begin in zip(row_refs, begins)], axis=0
    )
    together = count if count * tokens <= LANES else 1
    for base in range(0, count, together):
        gate = jnp.concatenate(found[base : base + together], axis=0)
        high = gate.astype(jnp.bfloat16)
        rest = (gate - high.astype(jnp.float32)).astype(jnp.bfloat16)
        both = jnp.dot(
            jnp.concatenate([high, rest], axis=0), rows, preferred_element_type=jnp.float32
        )
        half = together * tokens
        part = (both[:half] + both[half:]).astype(jnp.bfloat16)
        for d in range(together):
            out_refs[base + d][...] = part[d * tokens : (d + 1) * tokens]


def combine(chosen, rows, begins, low, capacity, after):
    count = len(chosen)
    tokens = chosen[0].shape[1]
    columns = rows[0].shape[1]
    return pl.pallas_call(
        functools.partial(combine_kernel, low, count, capacity, begins),
        out_shape=[shape_of((tokens, columns), jnp.bfloat16)] * count,
        in_specs=[VMEM] * (count + NODE_SIZE) + [ANY] * len(after),
        out_specs=[VMEM] * count,
        name="combine",
        cost_estimate=pl.CostEstimate(
            flops=4 * count * tokens * LANES * columns,
            bytes_accessed=4 * count * tokens * columns,
            transcendentals=0,
        ),
        compiler_params=pltpu.CompilerParams(vmem_limit_bytes=(40 if tokens > 16 else 8) * MIB),
    )(*chosen, *rows, *after)


def add_kernel(base_ref, *refs):
    total = base_ref[...].astype(jnp.float32)
    for ref in refs[:-1]:
        total = total + ref[...].astype(jnp.float32)
    refs[-1][...] = total


def add(base, parts):
    return pl.pallas_call(
        add_kernel,
        out_shape=shape_of(base.shape, jnp.float32),
        in_specs=[VMEM] * (1 + len(parts)),
        out_specs=VMEM,
        name="add",
        cost_estimate=pl.CostEstimate(
            flops=0, bytes_accessed=ADD_COST, transcendentals=0
        ),
        compiler_params=pltpu.CompilerParams(vmem_limit_bytes=(40 if base.shape[0] > 16 else 8) * MIB),
    )(base, *parts)


def fetch_kernel(columns, flip, source_hbm, after_ref, out_ref, pieces, sems):
    width = pieces.shape[2]
    base = (lax.axis_index("tensor") ^ flip) * columns
    copies = [
        pltpu.make_async_copy(
            source_hbm.at[:, pl.ds(pl.multiple_of(base + i * width, LANES), width)],
            pieces.at[i],
            sems.at[i],
        )
        for i in range(columns // width)
    ]
    for copy in copies:
        copy.start()
    for i, copy in enumerate(copies):
        copy.wait()
        out_ref[i * width : (i + 1) * width, :] = pieces[i].T


def fetch(source, columns, flip, after):
    width = block_width(columns)
    return pl.pallas_call(
        functools.partial(fetch_kernel, columns, flip),
        out_shape=pltpu.VMEM((columns, source.shape[0]), source.dtype),
        in_specs=[ANY, ANY],
        out_specs=VMEM,
        scratch_shapes=[
            pltpu.VMEM((columns // width, source.shape[0], width), source.dtype),
            pltpu.SemaphoreType.DMA((columns // width,)),
        ],
        name="fetch",
        cost_estimate=pl.CostEstimate(
            flops=0, bytes_accessed=2 * source.shape[0] * columns, transcendentals=0
        ),
        compiler_params=pltpu.CompilerParams(vmem_limit_bytes=40 * MIB),
    )(source, after)


def project_kernel(flip, block, carried, features, *refs):
    gain_ref, weight_ref, section_ref = refs[:3]
    refs = refs[3:]
    columns = section_ref.shape[1]
    base = lax.axis_index("tensor") ^ flip
    total = energy = None
    if carried:
        total, energy = refs[0][...], refs[1][...]
        refs = refs[2:]
    for i in range(0, columns, block):
        wide = section_ref[:, i : i + block].astype(jnp.float32)
        square = jnp.sum(wide * wide, axis=1, keepdims=True)
        begin = pl.multiple_of(base * columns + i, LANES)
        normed = (wide * gain_ref[:, pl.ds(begin, block)]).astype(jnp.bfloat16)
        product = lax.dot_general(
            normed,
            weight_ref[i : i + block, :],
            (((1,), (0,)), ((), ())),
            preferred_element_type=jnp.float32,
        )
        total = product if total is None else total + product
        energy = square if energy is None else energy + square
    if features:
        scale = lax.rsqrt(energy / features + epsilon)
        refs[0][...] = (total * scale).astype(jnp.bfloat16)
    else:
        refs[0][...] = total
        refs[1][...] = energy


def project(gain, weight, section, flip=0, carried=(), features=0):
    tokens, width = section.shape
    latents = weight.shape[1]
    block = width // 2 if width // 2 % LANES == 0 else width
    if features:
        out_shape = [shape_of((tokens, latents), jnp.bfloat16)]
    else:
        out_shape = [shape_of((tokens, latents), jnp.float32), shape_of((tokens, 1), jnp.float32)]
    return pl.pallas_call(
        functools.partial(project_kernel, flip, block, bool(carried), features),
        out_shape=out_shape,
        in_specs=[VMEM] * (3 + len(carried)),
        out_specs=[VMEM] * len(out_shape),
        name="project",
        cost_estimate=pl.CostEstimate(
            flops=64 * tokens * latents * width, bytes_accessed=0, transcendentals=0
        ),
        compiler_params=pltpu.CompilerParams(vmem_limit_bytes=8 * MIB),
    )(gain, weight, section, *carried)


def on_device(hidden, down_weight, expert_ids, gate_weights, residual, norm_gain, proj_weight):
    experts = lax.axis_size("expert")
    tensors = lax.axis_size("tensor")
    groups = experts // NODE_SIZE
    columns = down_weight.shape[2]
    capacity = hidden.shape[1] // experts
    features = columns * tensors
    spans = halves(groups)

    def swap(value, bits):
        return lax.ppermute(value, "expert", [(i, i ^ bits) for i in range(experts)])

    results = down(hidden, down_weight, experts, spans)
    results, expert_ids, gate_weights = lax.optimization_barrier(
        (results, expert_ids, gate_weights)
    )
    own, near, first, *rest = results
    first = swap(first, 2)
    near = swap(near, 1)
    rest = [swap(rows, 2 + n % 2) for n, rows in enumerate(rest)]
    chosen = [jnp.concatenate([expert_ids.T.astype(jnp.float32), gate_weights.T], axis=0)]
    while len(chosen) < groups:
        sent = jnp.concatenate(chosen, axis=0)
        got = swap(sent, len(chosen) * NODE_SIZE)
        chosen += jnp.split(got, len(chosen), axis=0)
    weight = proj_weight.T
    summed = residual
    begin = 0
    after = ()
    paired = columns % LANES == 0 and tensors == 2 and len(spans) == 2
    for n, (low, count) in enumerate(spans):
        height = count * capacity
        if n:
            far = rest[2 * n - 2 : 2 * n]
        else:
            far = [first, swap(first[height:], 1)]
        parts = combine(
            chosen[low : low + count],
            [own, near, *far],
            [begin, begin, 0, 0],
            low,
            capacity,
            after,
        )
        begin += height
        after = parts[:1]
        moved = [swap(part, d * NODE_SIZE) if d else part for d, part in enumerate(parts, low)]
        if low:
            summed = add(summed, moved)
        else:
            for part in moved:
                summed = summed.astype(jnp.float32) + part.astype(jnp.float32)
    stream = summed.astype(jnp.bfloat16)
    if not paired:
        wide = lax.all_gather(stream, "tensor", axis=1, tiled=True).astype(jnp.float32)
        normed = (wide * norm_gain).astype(jnp.bfloat16)
        added = jnp.dot(normed, proj_weight, preferred_element_type=jnp.float32)
        energy = jnp.sum(wide * wide, axis=1)
        inverse = lax.rsqrt(energy / features + epsilon)
        return (stream, (added * inverse[:, None]).astype(jnp.bfloat16))
    held = [fetch(weight, columns, flip, *after) for flip in range(2)]
    stream, held = lax.optimization_barrier((stream, held))
    other = lax.ppermute(stream, "tensor", [(i, i ^ 1) for i in range(tensors)])
    gain = norm_gain.reshape(1, features)
    carried = project(gain, held[0], stream)
    (latents,) = project(gain, held[1], other, 1, carried, features)
    return (stream, latents)


def solution(mesh):
    return jax.shard_map(
        on_device,
        mesh=mesh,
        in_specs=(
            P("expert", None, None),
            P("expert", None, "tensor"),
            P("expert", None),
            P("expert", None),
            P("expert", "tensor"),
            P(),
            P(None, "tensor"),
        ),
        out_specs=(P("expert", "tensor"), P("expert", "tensor")),
        check_vma=False,
    )
```

```python
import functools

import jax
import jax.numpy as jnp
from jax import lax
from jax.experimental import pallas as pl
from jax.experimental.pallas import tpu as pltpu
from jax.sharding import PartitionSpec as P

NODE_SIZE = 4
LANES = 128
MIB = 1 << 20
AHEAD = 3
DEPTH_STEPS = 8
ADD_COST = 64 * MIB


epsilon = 1e-06

VMEM = pl.BlockSpec(memory_space=pltpu.VMEM)
SMEM = pl.BlockSpec(memory_space=pltpu.SMEM)
ANY = pl.BlockSpec(memory_space=pl.ANY)
HBM = pl.BlockSpec(memory_space=pltpu.HBM)


def shape_of(shape, dtype):
    return jax.ShapeDtypeStruct(shape, dtype)


def block_width(width):
    for tiles in (4, 2, 3, 1):
        if width % (tiles * LANES) == 0:
            return tiles * LANES
    return width


def stages_of(groups):
    if groups % 4:
        return [list(range(groups))]
    quarter = groups // 4
    return [
        list(range(3 * quarter, groups)),
        list(range(2 * quarter, 3 * quarter)),
        list(range(2 * quarter)),
    ]


def pieces_of(stages):
    outputs = [[(j, d) for stage in stages for d in stage] for j in (0, 1)]
    for stage in stages[:-1] or stages:
        outputs.append([(j, d) for j in (2, 3) for d in stage])
    if len(stages) > 1:
        outputs += [[(j, d) for d in stages[-1]] for j in (2, 3)]
    return outputs


def down_kernel(experts, outputs, hidden_hbm, weight_hbm, *refs):
    out_refs = refs[: len(outputs)]
    hidden, wide, ordered, weights, total, hidden_sem, weight_sems = refs[len(outputs) :]
    index = lax.axis_index("expert")
    steps, depth = weights.shape[:2]
    first_copy = pltpu.make_async_copy(hidden_hbm.at[0], hidden, hidden_sem)
    copies = [
        pltpu.make_async_copy(
            weight_hbm.at[0, pl.ds(i * depth, depth)], weights.at[i], weight_sems.at[i]
        )
        for i in range(steps)
    ]
    first_copy.start()
    for copy in copies[:AHEAD]:
        copy.start()
    rows = hidden.shape[0]
    capacity = rows // experts
    first_copy.wait()
    wide[...] = hidden[...].astype(jnp.float32)
    order = [piece for pieces in outputs for piece in pieces]
    for n in range(0, len(order), 2):
        pair = []
        for j, d in order[n : n + 2]:
            owner = index ^ (d * NODE_SIZE + j)
            pair.append(wide[pl.ds(pl.multiple_of(owner * capacity, capacity), capacity), :])
        ordered[n * capacity : (n + 2) * capacity, :] = jnp.concatenate(pair, axis=0).astype(
            jnp.bfloat16
        )
    columns = total.shape[1]
    block = block_width(columns)
    for i, copy in enumerate(copies):
        copy.wait()
        if i + AHEAD < steps:
            copies[i + AHEAD].start()
        for first in range(0, columns, block):
            product = jnp.dot(
                ordered[:, i * depth : (i + 1) * depth],
                weights[i, :, first : first + block],
                preferred_element_type=jnp.float32,
            )
            if i:
                product = total[:, first : first + block] + product
            if i < steps - 1:
                total[:, first : first + block] = product
            else:
                begin = 0
                for ref in out_refs:
                    end = begin + ref.shape[0]
                    ref[:, first : first + block] = product[begin:end].astype(jnp.bfloat16)
                    begin = end


def down(hidden, down_weight, experts, stages):
    rows, depth = hidden.shape[1:]
    columns = down_weight.shape[2]
    capacity = rows // experts
    outputs = pieces_of(stages)
    out_shape = [shape_of((len(pieces) * capacity, columns), jnp.bfloat16) for pieces in outputs]
    return pl.pallas_call(
        functools.partial(down_kernel, experts, outputs),
        out_shape=out_shape,
        in_specs=[ANY, ANY],
        out_specs=[VMEM] * len(out_shape),
        scratch_shapes=[
            pltpu.VMEM((rows, depth), jnp.bfloat16),
            pltpu.VMEM((rows, depth), jnp.float32),
            pltpu.VMEM((rows, depth), jnp.bfloat16),
            pltpu.VMEM((DEPTH_STEPS, depth // DEPTH_STEPS, columns), jnp.bfloat16),
            pltpu.VMEM((rows, columns), jnp.float32),
            pltpu.SemaphoreType.DMA(()),
            pltpu.SemaphoreType.DMA((DEPTH_STEPS,)),
        ],
        name="down",
        cost_estimate=pl.CostEstimate(
            flops=2 * rows * depth * columns, bytes_accessed=2 * depth * columns, transcendentals=0
        ),
        compiler_params=pltpu.CompilerParams(vmem_limit_bytes=53 * MIB),
    )(hidden, down_weight)


def gates_of(index, low, count, capacity, tokens, chosen):
    shape = (NODE_SIZE * count * capacity, tokens)
    row = lax.broadcasted_iota(jnp.int32, shape, 0)
    slot = (row % capacity).astype(jnp.float32)
    group = row // capacity % count + low
    expert = (index ^ (row // (capacity * count))).astype(jnp.float32)
    earlier = lax.broadcasted_iota(jnp.int32, (tokens, tokens), 0) < lax.broadcasted_iota(
        jnp.int32, (tokens, tokens), 1
    )
    earlier = jnp.where(earlier, 1.0, 0.0)
    found = []
    for d in range(low, low + count):
        picks = chosen[d - low].shape[0] // 2
        ids, gates = chosen[d - low][:picks], chosen[d - low][picks:]
        named = jnp.zeros(shape, jnp.float32)
        gate = jnp.zeros(shape, jnp.float32)
        for k in range(picks):
            hit = ids[k : k + 1, :] == expert
            named = named + jnp.where(hit, 1.0, 0.0)
            gate = gate + jnp.where(hit, gates[k : k + 1, :], 0.0)
        before = jnp.dot(named, earlier, preferred_element_type=jnp.float32)
        found.append(jnp.where((before == slot) & (group == d), gate, 0.0).T)
    return found


def combine_kernel(low, count, capacity, begins, *refs):
    chosen_refs = refs[:count]
    row_refs = refs[count : count + NODE_SIZE]
    out_refs = refs[len(refs) - count :]
    tokens = chosen_refs[0].shape[1]
    index = lax.axis_index("expert")
    found = gates_of(index, low, count, capacity, tokens, [ref[...] for ref in chosen_refs])
    wide = [ref[...].astype(jnp.float32) for ref in row_refs]
    rows = jnp.concatenate(
        [rows[begin : begin + count * capacity] for rows, begin in zip(wide, begins)], axis=0
    ).astype(jnp.bfloat16)
    together = count if count * tokens <= LANES else 1
    for base in range(0, count, together):
        gate = jnp.concatenate(found[base : base + together], axis=0)
        high = gate.astype(jnp.bfloat16)
        rest = (gate - high.astype(jnp.float32)).astype(jnp.bfloat16)
        both = jnp.dot(
            jnp.concatenate([high, rest], axis=0), rows, preferred_element_type=jnp.float32
        )
        half = together * tokens
        part = (both[:half] + both[half:]).astype(jnp.bfloat16)
        for d in range(together):
            out_refs[base + d][...] = part[d * tokens : (d + 1) * tokens]


def combine(chosen, rows, begins, low, capacity, after):
    count = len(chosen)
    tokens = chosen[0].shape[1]
    columns = rows[0].shape[1]
    return pl.pallas_call(
        functools.partial(combine_kernel, low, count, capacity, begins),
        out_shape=[shape_of((tokens, columns), jnp.bfloat16)] * count,
        in_specs=[VMEM] * (count + NODE_SIZE) + [ANY] * len(after),
        out_specs=[VMEM] * count,
        name="combine",
        cost_estimate=pl.CostEstimate(
            flops=4 * count * tokens * LANES * columns,
            bytes_accessed=4 * count * tokens * columns,
            transcendentals=0,
        ),
        compiler_params=pltpu.CompilerParams(vmem_limit_bytes=(40 if tokens > 16 else 8) * MIB),
    )(*chosen, *rows, *after)


def add_kernel(base_ref, *refs):
    total = base_ref[...].astype(jnp.float32)
    for ref in refs[:-1]:
        total = total + ref[...].astype(jnp.float32)
    refs[-1][...] = total


def add(base, parts):
    return pl.pallas_call(
        add_kernel,
        out_shape=shape_of(base.shape, jnp.float32),
        in_specs=[VMEM] * (1 + len(parts)),
        out_specs=VMEM,
        name="add",
        cost_estimate=pl.CostEstimate(
            flops=0, bytes_accessed=ADD_COST, transcendentals=0
        ),
        compiler_params=pltpu.CompilerParams(vmem_limit_bytes=(40 if base.shape[0] > 16 else 8) * MIB),
    )(base, *parts)


def fetch_kernel(source_hbm, after_ref, out_ref, pieces, sems):
    count, _, width = pieces.shape
    copies = [
        pltpu.make_async_copy(
            source_hbm.at[:, pl.ds(i * width, width)], pieces.at[i], sems.at[i]
        )
        for i in range(count)
    ]
    for copy in copies:
        copy.start()
    for i, copy in enumerate(copies):
        copy.wait()
        out_ref[i * width : (i + 1) * width, :] = pieces[i].T


def fetch(source, after):
    rows, columns = source.shape
    width = block_width(columns)
    return pl.pallas_call(
        fetch_kernel,
        out_shape=pltpu.VMEM((columns, rows), source.dtype),
        in_specs=[ANY, ANY],
        out_specs=VMEM,
        scratch_shapes=[
            pltpu.VMEM((columns // width, rows, width), source.dtype),
            pltpu.SemaphoreType.DMA((columns // width,)),
        ],
        name="fetch",
        cost_estimate=pl.CostEstimate(
            flops=0, bytes_accessed=2 * source.size, transcendentals=0
        ),
        compiler_params=pltpu.CompilerParams(vmem_limit_bytes=40 * MIB),
    )(source, after)


def project_kernel(flip, block, carried, features, *refs):
    gain_ref, weight_ref, section_ref = refs[:3]
    refs = refs[3:]
    columns = section_ref.shape[1]
    base = lax.axis_index("tensor") ^ flip
    total = energy = None
    if carried:
        total, energy = refs[0][...], refs[1][...]
        refs = refs[2:]
    for i in range(0, columns, block):
        wide = section_ref[:, i : i + block].astype(jnp.float32)
        square = jnp.sum(wide * wide, axis=1, keepdims=True)
        begin = pl.multiple_of(base * columns + i, LANES)
        normed = (wide * gain_ref[:, pl.ds(begin, block)]).astype(jnp.bfloat16)
        product = lax.dot_general(
            normed,
            weight_ref[pl.ds(begin, block), :],
            (((1,), (0,)), ((), ())),
            preferred_element_type=jnp.float32,
        )
        total = product if total is None else total + product
        energy = square if energy is None else energy + square
    if features:
        scale = lax.rsqrt(energy / features + epsilon)
        refs[0][...] = (total * scale).astype(jnp.bfloat16)
    else:
        refs[0][...] = total
        refs[1][...] = energy


def project(gain, weight, section, flip=0, carried=(), features=0):
    tokens, width = section.shape
    latents = weight.shape[1]
    block = width // 2 if width // 2 % LANES == 0 else width
    if features:
        out_shape = [shape_of((tokens, latents), jnp.bfloat16)]
    else:
        out_shape = [shape_of((tokens, latents), jnp.float32), shape_of((tokens, 1), jnp.float32)]
    return pl.pallas_call(
        functools.partial(project_kernel, flip, block, bool(carried), features),
        out_shape=out_shape,
        in_specs=[VMEM] * (3 + len(carried)),
        out_specs=[VMEM] * len(out_shape),
        name="project",
        cost_estimate=pl.CostEstimate(
            flops=64 * tokens * latents * width, bytes_accessed=0, transcendentals=0
        ),
        compiler_params=pltpu.CompilerParams(vmem_limit_bytes=8 * MIB),
    )(gain, weight, section, *carried)


def on_device(hidden, down_weight, expert_ids, gate_weights, residual, norm_gain, proj_weight):
    experts = lax.axis_size("expert")
    tensors = lax.axis_size("tensor")
    groups = experts // NODE_SIZE
    columns = down_weight.shape[2]
    capacity = hidden.shape[1] // experts
    features = columns * tensors
    stages = stages_of(groups)

    def swap(value, bits):
        return lax.ppermute(value, "expert", [(i, i ^ bits) for i in range(experts)])

    results = down(hidden, down_weight, experts, stages)
    results, expert_ids, gate_weights = lax.optimization_barrier(
        (results, expert_ids, gate_weights)
    )
    own, near, *far = results
    early = max(len(stages) - 1, 1)
    far[:early] = [swap(rows, 2) for rows in far[:early]]
    near = swap(near, 1)
    far[0], *far[early:] = lax.optimization_barrier((far[0], *far[early:]))
    far[early:] = [swap(rows, 2 + n) for n, rows in enumerate(far[early:])]
    chosen = [jnp.concatenate([expert_ids.T.astype(jnp.float32), gate_weights.T], axis=0)]
    while len(chosen) < groups:
        sent = jnp.concatenate(chosen, axis=0)
        got = swap(sent, len(chosen) * NODE_SIZE)
        chosen += jnp.split(got, len(chosen), axis=0)
    weight = proj_weight.T
    summed = residual
    begin = 0
    after = ()
    paired = columns % LANES == 0 and tensors == 2
    for n, stage in enumerate(stages):
        height = len(stage) * capacity
        if n < early:
            rows = [far[n], swap(far[n][height:], 1)]
        else:
            rows = far[early:]
        parts = combine(
            [chosen[d] for d in stage],
            [own, near, *rows],
            [begin, begin, 0, 0],
            stage[0],
            capacity,
            after,
        )
        begin += height
        after = parts[:1]
        moved = [swap(part, d * NODE_SIZE) if d else part for d, part in zip(stage, parts)]
        if n < early and len(stages) > 1:
            summed = add(summed, moved)
        else:
            for part in moved:
                summed = summed.astype(jnp.float32) + part.astype(jnp.float32)
    stream = summed.astype(jnp.bfloat16)
    if not paired:
        wide = lax.all_gather(stream, "tensor", axis=1, tiled=True).astype(jnp.float32)
        normed = (wide * norm_gain).astype(jnp.bfloat16)
        added = jnp.dot(normed, proj_weight, preferred_element_type=jnp.float32)
        energy = jnp.sum(wide * wide, axis=1)
        inverse = lax.rsqrt(energy / features + epsilon)
        return (stream, (added * inverse[:, None]).astype(jnp.bfloat16))
    held = fetch(weight, *after)
    stream, held = lax.optimization_barrier((stream, held))
    other = lax.ppermute(stream, "tensor", [(i, i ^ 1) for i in range(tensors)])
    gain = norm_gain.reshape(1, features)
    carried = project(gain, held, stream)
    (latents,) = project(gain, held, other, 1, carried, features)
    return (stream, latents)


def solution(mesh):
    return jax.shard_map(
        on_device,
        mesh=mesh,
        in_specs=(
            P("expert", None, None),
            P("expert", None, "tensor"),
            P("expert", None),
            P("expert", None),
            P("expert", "tensor"),
            P(),
            P(None, "tensor"),
        ),
        out_specs=(P("expert", "tensor"), P("expert", "tensor")),
        check_vma=False,
    )
```

```python
import functools

import jax
import jax.numpy as jnp
from jax import lax
from jax.experimental import pallas as pl
from jax.experimental.pallas import tpu as pltpu
from jax.sharding import PartitionSpec as P

NODE_SIZE = 4
LANES = 128
MIB = 1 << 20
AHEAD = 3
DEPTH_PARTS = (4, 4, 4, 2, 2)
ADD_COST = 64 * MIB


epsilon = 1e-06

VMEM = pl.BlockSpec(memory_space=pltpu.VMEM)
SMEM = pl.BlockSpec(memory_space=pltpu.SMEM)
ANY = pl.BlockSpec(memory_space=pl.ANY)
HBM = pl.BlockSpec(memory_space=pltpu.HBM)


def shape_of(shape, dtype):
    return jax.ShapeDtypeStruct(shape, dtype)


def block_width(width):
    for tiles in (4, 2, 3, 1):
        if width % (tiles * LANES) == 0:
            return tiles * LANES
    return width


def stages_of(groups):
    if groups % 4:
        return [list(range(groups))]
    quarter = groups // 4
    return [
        list(range(3 * quarter, groups)),
        list(range(2 * quarter, 3 * quarter)),
        list(range(2 * quarter)),
    ]


def pieces_of(stages):
    outputs = [[(j, d) for stage in stages for d in stage] for j in (0, 1)]
    for stage in stages[:-1] or stages:
        outputs.append([(j, d) for j in (2, 3) for d in stage])
    if len(stages) > 1:
        outputs += [[(j, d) for d in stages[-1]] for j in (2, 3)]
    return outputs


def down_kernel(experts, outputs, hidden_hbm, weight_hbm, *refs):
    out_refs = refs[: len(outputs)]
    hidden, wide, ordered, weights, total, hidden_sem, weight_sems = refs[len(outputs) :]
    index = lax.axis_index("expert")
    unit = weights.shape[0] // sum(DEPTH_PARTS)
    bounds = [sum(DEPTH_PARTS[:n]) * unit for n in range(len(DEPTH_PARTS) + 1)]
    steps = len(DEPTH_PARTS)
    first_copy = pltpu.make_async_copy(hidden_hbm.at[0], hidden, hidden_sem)
    copies = [
        pltpu.make_async_copy(
            weight_hbm.at[0, pl.ds(bounds[i], bounds[i + 1] - bounds[i])],
            weights.at[pl.ds(bounds[i], bounds[i + 1] - bounds[i])],
            weight_sems.at[i],
        )
        for i in range(steps)
    ]
    first_copy.start()
    for copy in copies[:AHEAD]:
        copy.start()
    rows = hidden.shape[0]
    capacity = rows // experts
    first_copy.wait()
    wide[...] = hidden[...].astype(jnp.float32)
    order = [piece for pieces in outputs for piece in pieces]
    for n in range(0, len(order), 2):
        pair = []
        for j, d in order[n : n + 2]:
            owner = index ^ (d * NODE_SIZE + j)
            pair.append(wide[pl.ds(pl.multiple_of(owner * capacity, capacity), capacity), :])
        ordered[n * capacity : (n + 2) * capacity, :] = jnp.concatenate(pair, axis=0).astype(
            jnp.bfloat16
        )
    columns = total.shape[1]
    block = block_width(columns)
    for i, copy in enumerate(copies):
        copy.wait()
        if i + AHEAD < steps:
            copies[i + AHEAD].start()
        for first in range(0, columns, block):
            product = jnp.dot(
                ordered[:, bounds[i] : bounds[i + 1]],
                weights[bounds[i] : bounds[i + 1], first : first + block],
                preferred_element_type=jnp.float32,
            )
            if i:
                product = total[:, first : first + block] + product
            if i < steps - 1:
                total[:, first : first + block] = product
            else:
                begin = 0
                for ref in out_refs:
                    end = begin + ref.shape[0]
                    ref[:, first : first + block] = product[begin:end].astype(jnp.bfloat16)
                    begin = end


def down(hidden, down_weight, experts, stages):
    rows, depth = hidden.shape[1:]
    columns = down_weight.shape[2]
    capacity = rows // experts
    outputs = pieces_of(stages)
    out_shape = [shape_of((len(pieces) * capacity, columns), jnp.bfloat16) for pieces in outputs]
    return pl.pallas_call(
        functools.partial(down_kernel, experts, outputs),
        out_shape=out_shape,
        in_specs=[ANY, ANY],
        out_specs=[VMEM] * len(out_shape),
        scratch_shapes=[
            pltpu.VMEM((rows, depth), jnp.bfloat16),
            pltpu.VMEM((rows, depth), jnp.float32),
            pltpu.VMEM((rows, depth), jnp.bfloat16),
            pltpu.VMEM((depth, columns), jnp.bfloat16),
            pltpu.VMEM((rows, columns), jnp.float32),
            pltpu.SemaphoreType.DMA(()),
            pltpu.SemaphoreType.DMA((len(DEPTH_PARTS),)),
        ],
        name="down",
        cost_estimate=pl.CostEstimate(
            flops=2 * rows * depth * columns, bytes_accessed=2 * depth * columns, transcendentals=0
        ),
        compiler_params=pltpu.CompilerParams(vmem_limit_bytes=53 * MIB),
    )(hidden, down_weight)


def gates_of(index, low, count, capacity, tokens, chosen):
    shape = (NODE_SIZE * count * capacity, tokens)
    row = lax.broadcasted_iota(jnp.int32, shape, 0)
    slot = (row % capacity).astype(jnp.float32)
    group = row // capacity % count + low
    expert = (index ^ (row // (capacity * count))).astype(jnp.float32)
    earlier = lax.broadcasted_iota(jnp.int32, (tokens, tokens), 0) < lax.broadcasted_iota(
        jnp.int32, (tokens, tokens), 1
    )
    earlier = jnp.where(earlier, 1.0, 0.0)
    found = []
    for d in range(low, low + count):
        picks = chosen[d - low].shape[0] // 2
        ids, gates = chosen[d - low][:picks], chosen[d - low][picks:]
        named = jnp.zeros(shape, jnp.float32)
        gate = jnp.zeros(shape, jnp.float32)
        for k in range(picks):
            hit = ids[k : k + 1, :] == expert
            named = named + jnp.where(hit, 1.0, 0.0)
            gate = gate + jnp.where(hit, gates[k : k + 1, :], 0.0)
        before = jnp.dot(named, earlier, preferred_element_type=jnp.float32)
        found.append(jnp.where((before == slot) & (group == d), gate, 0.0).T)
    return found


def combine_kernel(low, count, capacity, begins, *refs):
    chosen_refs = refs[:count]
    row_refs = refs[count : count + NODE_SIZE]
    out_refs = refs[len(refs) - count :]
    tokens = chosen_refs[0].shape[1]
    index = lax.axis_index("expert")
    found = gates_of(index, low, count, capacity, tokens, [ref[...] for ref in chosen_refs])
    wide = [ref[...].astype(jnp.float32) for ref in row_refs]
    rows = jnp.concatenate(
        [rows[begin : begin + count * capacity] for rows, begin in zip(wide, begins)], axis=0
    ).astype(jnp.bfloat16)
    together = count if count * tokens <= LANES else 1
    for base in range(0, count, together):
        gate = jnp.concatenate(found[base : base + together], axis=0)
        high = gate.astype(jnp.bfloat16)
        rest = (gate - high.astype(jnp.float32)).astype(jnp.bfloat16)
        both = jnp.dot(
            jnp.concatenate([high, rest], axis=0), rows, preferred_element_type=jnp.float32
        )
        half = together * tokens
        part = (both[:half] + both[half:]).astype(jnp.bfloat16)
        for d in range(together):
            out_refs[base + d][...] = part[d * tokens : (d + 1) * tokens]


def combine(chosen, rows, begins, low, capacity, after):
    count = len(chosen)
    tokens = chosen[0].shape[1]
    columns = rows[0].shape[1]
    return pl.pallas_call(
        functools.partial(combine_kernel, low, count, capacity, begins),
        out_shape=[shape_of((tokens, columns), jnp.bfloat16)] * count,
        in_specs=[VMEM] * (count + NODE_SIZE) + [ANY] * len(after),
        out_specs=[VMEM] * count,
        name="combine",
        cost_estimate=pl.CostEstimate(
            flops=4 * count * tokens * LANES * columns,
            bytes_accessed=4 * count * tokens * columns,
            transcendentals=0,
        ),
        compiler_params=pltpu.CompilerParams(vmem_limit_bytes=(40 if tokens > 16 else 8) * MIB),
    )(*chosen, *rows, *after)


def add_kernel(base_ref, *refs):
    total = base_ref[...].astype(jnp.float32)
    for ref in refs[:-1]:
        total = total + ref[...].astype(jnp.float32)
    refs[-1][...] = total


def add(base, parts):
    return pl.pallas_call(
        add_kernel,
        out_shape=shape_of(base.shape, jnp.float32),
        in_specs=[VMEM] * (1 + len(parts)),
        out_specs=VMEM,
        name="add",
        cost_estimate=pl.CostEstimate(
            flops=0, bytes_accessed=ADD_COST, transcendentals=0
        ),
        compiler_params=pltpu.CompilerParams(vmem_limit_bytes=(40 if base.shape[0] > 16 else 8) * MIB),
    )(base, *parts)


def fetch_kernel(source_hbm, after_ref, out_ref, pieces, sems):
    count, _, width = pieces.shape
    copies = [
        pltpu.make_async_copy(
            source_hbm.at[:, pl.ds(i * width, width)], pieces.at[i], sems.at[i]
        )
        for i in range(count)
    ]
    for copy in copies:
        copy.start()
    for i, copy in enumerate(copies):
        copy.wait()
        out_ref[i * width : (i + 1) * width, :] = pieces[i].T


def fetch(source, after):
    rows, columns = source.shape
    width = block_width(columns)
    return pl.pallas_call(
        fetch_kernel,
        out_shape=pltpu.VMEM((columns, rows), source.dtype),
        in_specs=[ANY, ANY],
        out_specs=VMEM,
        scratch_shapes=[
            pltpu.VMEM((columns // width, rows, width), source.dtype),
            pltpu.SemaphoreType.DMA((columns // width,)),
        ],
        name="fetch",
        cost_estimate=pl.CostEstimate(
            flops=0, bytes_accessed=2 * source.size, transcendentals=0
        ),
        compiler_params=pltpu.CompilerParams(vmem_limit_bytes=32 * MIB),
    )(source, after)


def project_kernel(flip, block, carried, features, *refs):
    gain_ref, weight_ref, section_ref = refs[:3]
    refs = refs[3:]
    columns = section_ref.shape[1]
    base = lax.axis_index("tensor") ^ flip
    total = energy = None
    if carried:
        total, energy = refs[0][...], refs[1][...]
        refs = refs[2:]
    for i in range(0, columns, block):
        wide = section_ref[:, i : i + block].astype(jnp.float32)
        square = jnp.sum(wide * wide, axis=1, keepdims=True)
        begin = pl.multiple_of(base * columns + i, LANES)
        normed = (wide * gain_ref[:, pl.ds(begin, block)]).astype(jnp.bfloat16)
        product = lax.dot_general(
            normed,
            weight_ref[pl.ds(begin, block), :],
            (((1,), (0,)), ((), ())),
            preferred_element_type=jnp.float32,
        )
        total = product if total is None else total + product
        energy = square if energy is None else energy + square
    if features:
        scale = lax.rsqrt(energy / features + epsilon)
        refs[0][...] = (total * scale).astype(jnp.bfloat16)
    else:
        refs[0][...] = total
        refs[1][...] = energy


def project(gain, weight, section, flip=0, carried=(), features=0):
    tokens, width = section.shape
    latents = weight.shape[1]
    block = width // 2 if width // 2 % LANES == 0 else width
    if features:
        out_shape = [shape_of((tokens, latents), jnp.bfloat16)]
    else:
        out_shape = [shape_of((tokens, latents), jnp.float32), shape_of((tokens, 1), jnp.float32)]
    return pl.pallas_call(
        functools.partial(project_kernel, flip, block, bool(carried), features),
        out_shape=out_shape,
        in_specs=[VMEM] * (3 + len(carried)),
        out_specs=[VMEM] * len(out_shape),
        name="project",
        cost_estimate=pl.CostEstimate(
            flops=64 * tokens * latents * width, bytes_accessed=0, transcendentals=0
        ),
        compiler_params=pltpu.CompilerParams(vmem_limit_bytes=8 * MIB),
    )(gain, weight, section, *carried)


def on_device(hidden, down_weight, expert_ids, gate_weights, residual, norm_gain, proj_weight):
    experts = lax.axis_size("expert")
    tensors = lax.axis_size("tensor")
    groups = experts // NODE_SIZE
    columns = down_weight.shape[2]
    capacity = hidden.shape[1] // experts
    features = columns * tensors
    stages = stages_of(groups)

    def swap(value, bits):
        return lax.ppermute(value, "expert", [(i, i ^ bits) for i in range(experts)])

    results = down(hidden, down_weight, experts, stages)
    results, expert_ids, gate_weights = lax.optimization_barrier(
        (results, expert_ids, gate_weights)
    )
    own, near, *far = results
    early = max(len(stages) - 1, 1)
    far[:early] = [swap(rows, 2) for rows in far[:early]]
    near = swap(near, 1)
    far[0], *far[early:] = lax.optimization_barrier((far[0], *far[early:]))
    far[early:] = [swap(rows, 2 + n) for n, rows in enumerate(far[early:])]
    chosen = [jnp.concatenate([expert_ids.T.astype(jnp.float32), gate_weights.T], axis=0)]
    while len(chosen) < groups:
        sent = jnp.concatenate(chosen, axis=0)
        got = swap(sent, len(chosen) * NODE_SIZE)
        chosen += jnp.split(got, len(chosen), axis=0)
    weight = proj_weight.T
    summed = residual
    begin = 0
    after = ()
    paired = columns % LANES == 0 and tensors == 2
    for n, stage in enumerate(stages):
        height = len(stage) * capacity
        if n < early:
            rows = [far[n], swap(far[n][height:], 1)]
        else:
            rows = far[early:]
        parts = combine(
            [chosen[d] for d in stage],
            [own, near, *rows],
            [begin, begin, 0, 0],
            stage[0],
            capacity,
            after,
        )
        begin += height
        after = parts[:1]
        moved = [swap(part, d * NODE_SIZE) if d else part for d, part in zip(stage, parts)]
        if n < early and len(stages) > 1:
            summed = add(summed, moved)
        else:
            for part in moved:
                summed = summed.astype(jnp.float32) + part.astype(jnp.float32)
    stream = summed.astype(jnp.bfloat16)
    if not paired:
        wide = lax.all_gather(stream, "tensor", axis=1, tiled=True).astype(jnp.float32)
        normed = (wide * norm_gain).astype(jnp.bfloat16)
        added = jnp.dot(normed, proj_weight, preferred_element_type=jnp.float32)
        energy = jnp.sum(wide * wide, axis=1)
        inverse = lax.rsqrt(energy / features + epsilon)
        return (stream, (added * inverse[:, None]).astype(jnp.bfloat16))
    held = fetch(weight, *after)
    stream, held = lax.optimization_barrier((stream, held))
    other = lax.ppermute(stream, "tensor", [(i, i ^ 1) for i in range(tensors)])
    gain = norm_gain.reshape(1, features)
    carried = project(gain, held, stream)
    (latents,) = project(gain, held, other, 1, carried, features)
    return (stream, latents)


def solution(mesh):
    return jax.shard_map(
        on_device,
        mesh=mesh,
        in_specs=(
            P("expert", None, None),
            P("expert", None, "tensor"),
            P("expert", None),
            P("expert", None),
            P("expert", "tensor"),
            P(),
            P(None, "tensor"),
        ),
        out_specs=(P("expert", "tensor"), P("expert", "tensor")),
        check_vma=False,
    )
```

```python
import functools

import jax
import jax.numpy as jnp
from jax import lax
from jax.experimental import pallas as pl
from jax.experimental.pallas import tpu as pltpu
from jax.sharding import PartitionSpec as P

NODE_SIZE = 4
LANES = 128
MIB = 1 << 20
AHEAD = 3
DEPTH_PARTS = (4, 4, 4, 2, 2)
ADD_COST = 64 * MIB


epsilon = 1e-06

VMEM = pl.BlockSpec(memory_space=pltpu.VMEM)
SMEM = pl.BlockSpec(memory_space=pltpu.SMEM)
ANY = pl.BlockSpec(memory_space=pl.ANY)
HBM = pl.BlockSpec(memory_space=pltpu.HBM)


def shape_of(shape, dtype):
    return jax.ShapeDtypeStruct(shape, dtype)


def block_width(width):
    for tiles in (4, 2, 3, 1):
        if width % (tiles * LANES) == 0:
            return tiles * LANES
    return width


def stages_of(groups):
    if groups % 4:
        return [list(range(groups))]
    quarter = groups // 4
    return [
        list(range(3 * quarter, groups)),
        list(range(2 * quarter, 3 * quarter)),
        list(range(2 * quarter)),
    ]


def pieces_of(stages):
    outputs = [[(j, d) for stage in stages for d in stage] for j in (0, 1)]
    for stage in stages[:-1] or stages:
        outputs.append([(j, d) for j in (2, 3) for d in stage])
    if len(stages) > 1:
        outputs += [[(j, d) for d in stages[-1]] for j in (2, 3)]
    return outputs


def down_kernel(experts, outputs, hidden_hbm, weight_hbm, *refs):
    out_refs = refs[: len(outputs)]
    hidden, wide, ordered, weights, total, hidden_sem, weight_sems = refs[len(outputs) :]
    index = lax.axis_index("expert")
    unit = weights.shape[0] // sum(DEPTH_PARTS)
    bounds = [sum(DEPTH_PARTS[:n]) * unit for n in range(len(DEPTH_PARTS) + 1)]
    steps = len(DEPTH_PARTS)
    first_copy = pltpu.make_async_copy(hidden_hbm.at[0], hidden, hidden_sem)
    copies = [
        pltpu.make_async_copy(
            weight_hbm.at[0, pl.ds(bounds[i], bounds[i + 1] - bounds[i])],
            weights.at[pl.ds(bounds[i], bounds[i + 1] - bounds[i])],
            weight_sems.at[i],
        )
        for i in range(steps)
    ]
    first_copy.start()
    for copy in copies[:AHEAD]:
        copy.start()
    rows = hidden.shape[0]
    capacity = rows // experts
    first_copy.wait()
    wide[...] = hidden[...].astype(jnp.float32)
    order = [piece for pieces in outputs for piece in pieces]
    for n in range(0, len(order), 2):
        pair = []
        for j, d in order[n : n + 2]:
            owner = index ^ (d * NODE_SIZE + j)
            pair.append(wide[pl.ds(pl.multiple_of(owner * capacity, capacity), capacity), :])
        ordered[n * capacity : (n + 2) * capacity, :] = jnp.concatenate(pair, axis=0).astype(
            jnp.bfloat16
        )
    columns = total.shape[1]
    block = columns // 2 if columns % (2 * LANES) == 0 else block_width(columns)
    for i, copy in enumerate(copies):
        copy.wait()
        if i + AHEAD < steps:
            copies[i + AHEAD].start()
        for first in range(0, columns, block):
            product = jnp.dot(
                ordered[:, bounds[i] : bounds[i + 1]],
                weights[bounds[i] : bounds[i + 1], first : first + block],
                preferred_element_type=jnp.float32,
            )
            if i:
                product = total[:, first : first + block] + product
            if i < steps - 1:
                total[:, first : first + block] = product
            else:
                begin = 0
                for ref in out_refs:
                    end = begin + ref.shape[0]
                    ref[:, first : first + block] = product[begin:end].astype(jnp.bfloat16)
                    begin = end


def down(hidden, down_weight, experts, stages):
    rows, depth = hidden.shape[1:]
    columns = down_weight.shape[2]
    capacity = rows // experts
    outputs = pieces_of(stages)
    out_shape = [shape_of((len(pieces) * capacity, columns), jnp.bfloat16) for pieces in outputs]
    return pl.pallas_call(
        functools.partial(down_kernel, experts, outputs),
        out_shape=out_shape,
        in_specs=[ANY, ANY],
        out_specs=[VMEM] * len(out_shape),
        scratch_shapes=[
            pltpu.VMEM((rows, depth), jnp.bfloat16),
            pltpu.VMEM((rows, depth), jnp.float32),
            pltpu.VMEM((rows, depth), jnp.bfloat16),
            pltpu.VMEM((depth, columns), jnp.bfloat16),
            pltpu.VMEM((rows, columns), jnp.float32),
            pltpu.SemaphoreType.DMA(()),
            pltpu.SemaphoreType.DMA((len(DEPTH_PARTS),)),
        ],
        name="down",
        cost_estimate=pl.CostEstimate(
            flops=2 * rows * depth * columns, bytes_accessed=2 * depth * columns, transcendentals=0
        ),
        compiler_params=pltpu.CompilerParams(vmem_limit_bytes=53 * MIB),
    )(hidden, down_weight)


def gates_of(index, low, count, capacity, tokens, chosen):
    shape = (NODE_SIZE * count * capacity, tokens)
    row = lax.broadcasted_iota(jnp.int32, shape, 0)
    slot = (row % capacity).astype(jnp.float32)
    group = row // capacity % count + low
    expert = (index ^ (row // (capacity * count))).astype(jnp.float32)
    earlier = lax.broadcasted_iota(jnp.int32, (tokens, tokens), 0) < lax.broadcasted_iota(
        jnp.int32, (tokens, tokens), 1
    )
    earlier = jnp.where(earlier, 1.0, 0.0)
    found = []
    for d in range(low, low + count):
        picks = chosen[d - low].shape[0] // 2
        ids, gates = chosen[d - low][:picks], chosen[d - low][picks:]
        named = jnp.zeros(shape, jnp.float32)
        gate = jnp.zeros(shape, jnp.float32)
        for k in range(picks):
            hit = ids[k : k + 1, :] == expert
            named = named + jnp.where(hit, 1.0, 0.0)
            gate = gate + jnp.where(hit, gates[k : k + 1, :], 0.0)
        before = jnp.dot(named, earlier, preferred_element_type=jnp.float32)
        found.append(jnp.where((before == slot) & (group == d), gate, 0.0).T)
    return found


def combine_kernel(low, count, capacity, begins, *refs):
    chosen_refs = refs[:count]
    row_refs = refs[count : count + NODE_SIZE]
    out_refs = refs[len(refs) - count :]
    tokens = chosen_refs[0].shape[1]
    index = lax.axis_index("expert")
    found = gates_of(index, low, count, capacity, tokens, [ref[...] for ref in chosen_refs])
    picked = []
    for ref, begin in zip(row_refs, begins):
        end = begin + count * capacity
        low_row, high_row = begin // 16 * 16, min(-(-end // 16) * 16, ref.shape[0])
        wide = ref[low_row:high_row].astype(jnp.float32)
        picked.append(wide[begin - low_row : end - low_row])
    rows = jnp.concatenate(picked, axis=0).astype(jnp.bfloat16)
    together = count if count * tokens <= LANES else 1
    for base in range(0, count, together):
        gate = jnp.concatenate(found[base : base + together], axis=0)
        high = gate.astype(jnp.bfloat16)
        rest = (gate - high.astype(jnp.float32)).astype(jnp.bfloat16)
        both = jnp.dot(
            jnp.concatenate([high, rest], axis=0), rows, preferred_element_type=jnp.float32
        )
        half = together * tokens
        part = (both[:half] + both[half:]).astype(jnp.bfloat16)
        for d in range(together):
            out_refs[base + d][...] = part[d * tokens : (d + 1) * tokens]


def combine(chosen, rows, begins, low, capacity, after):
    count = len(chosen)
    tokens = chosen[0].shape[1]
    columns = rows[0].shape[1]
    return pl.pallas_call(
        functools.partial(combine_kernel, low, count, capacity, begins),
        out_shape=[shape_of((tokens, columns), jnp.bfloat16)] * count,
        in_specs=[VMEM] * (count + NODE_SIZE) + [ANY] * len(after),
        out_specs=[VMEM] * count,
        name="combine",
        cost_estimate=pl.CostEstimate(
            flops=4 * count * tokens * LANES * columns,
            bytes_accessed=4 * count * tokens * columns,
            transcendentals=0,
        ),
        compiler_params=pltpu.CompilerParams(vmem_limit_bytes=(40 if tokens > 16 else 8) * MIB),
    )(*chosen, *rows, *after)


def add_kernel(base_ref, *refs):
    total = base_ref[...].astype(jnp.float32)
    for ref in refs[:-1]:
        total = total + ref[...].astype(jnp.float32)
    refs[-1][...] = total


def add(base, parts):
    return pl.pallas_call(
        add_kernel,
        out_shape=shape_of(base.shape, jnp.float32),
        in_specs=[VMEM] * (1 + len(parts)),
        out_specs=VMEM,
        name="add",
        cost_estimate=pl.CostEstimate(
            flops=0, bytes_accessed=ADD_COST, transcendentals=0
        ),
        compiler_params=pltpu.CompilerParams(vmem_limit_bytes=(40 if base.shape[0] > 16 else 8) * MIB),
    )(base, *parts)


def fetch_kernel(source_hbm, after_ref, out_ref, pieces, sems):
    count, _, width = pieces.shape
    copies = [
        pltpu.make_async_copy(
            source_hbm.at[:, pl.ds(i * width, width)], pieces.at[i], sems.at[i]
        )
        for i in range(count)
    ]
    for copy in copies:
        copy.start()
    for i, copy in enumerate(copies):
        copy.wait()
        out_ref[i * width : (i + 1) * width, :] = pieces[i].T


def fetch(source, after):
    rows, columns = source.shape
    width = block_width(columns)
    return pl.pallas_call(
        fetch_kernel,
        out_shape=pltpu.VMEM((columns, rows), source.dtype),
        in_specs=[ANY, ANY],
        out_specs=VMEM,
        scratch_shapes=[
            pltpu.VMEM((columns // width, rows, width), source.dtype),
            pltpu.SemaphoreType.DMA((columns // width,)),
        ],
        name="fetch",
        cost_estimate=pl.CostEstimate(
            flops=0, bytes_accessed=2 * source.size, transcendentals=0
        ),
        compiler_params=pltpu.CompilerParams(vmem_limit_bytes=32 * MIB),
    )(source, after)


def project_kernel(flip, block, carried, features, *refs):
    gain_ref, weight_ref, section_ref = refs[:3]
    refs = refs[3:]
    columns = section_ref.shape[1]
    base = lax.axis_index("tensor") ^ flip
    total = energy = None
    if carried:
        total, energy = refs[0][...], refs[1][...]
        refs = refs[2:]
    for i in range(0, columns, block):
        wide = section_ref[:, i : i + block].astype(jnp.float32)
        square = jnp.sum(wide * wide, axis=1, keepdims=True)
        begin = pl.multiple_of(base * columns + i, LANES)
        normed = (wide * gain_ref[:, pl.ds(begin, block)]).astype(jnp.bfloat16)
        product = lax.dot_general(
            normed,
            weight_ref[pl.ds(begin, block), :],
            (((1,), (0,)), ((), ())),
            preferred_element_type=jnp.float32,
        )
        total = product if total is None else total + product
        energy = square if energy is None else energy + square
    if features:
        scale = lax.rsqrt(energy / features + epsilon)
        refs[0][...] = (total * scale).astype(jnp.bfloat16)
    else:
        refs[0][...] = total
        refs[1][...] = energy


def project(gain, weight, section, flip=0, carried=(), features=0):
    tokens, width = section.shape
    latents = weight.shape[1]
    block = width // 2 if width // 2 % LANES == 0 else width
    if features:
        out_shape = [shape_of((tokens, latents), jnp.bfloat16)]
    else:
        out_shape = [shape_of((tokens, latents), jnp.float32), shape_of((tokens, 1), jnp.float32)]
    return pl.pallas_call(
        functools.partial(project_kernel, flip, block, bool(carried), features),
        out_shape=out_shape,
        in_specs=[VMEM] * (3 + len(carried)),
        out_specs=[VMEM] * len(out_shape),
        name="project",
        cost_estimate=pl.CostEstimate(
            flops=64 * tokens * latents * width, bytes_accessed=0, transcendentals=0
        ),
        compiler_params=pltpu.CompilerParams(vmem_limit_bytes=8 * MIB),
    )(gain, weight, section, *carried)


def on_device(hidden, down_weight, expert_ids, gate_weights, residual, norm_gain, proj_weight):
    experts = lax.axis_size("expert")
    tensors = lax.axis_size("tensor")
    groups = experts // NODE_SIZE
    columns = down_weight.shape[2]
    capacity = hidden.shape[1] // experts
    features = columns * tensors
    stages = stages_of(groups)

    def swap(value, bits):
        return lax.ppermute(value, "expert", [(i, i ^ bits) for i in range(experts)])

    results = down(hidden, down_weight, experts, stages)
    results, expert_ids, gate_weights = lax.optimization_barrier(
        (results, expert_ids, gate_weights)
    )
    own, near, *far = results
    early = max(len(stages) - 1, 1)
    far[:early] = [swap(rows, 2) for rows in far[:early]]
    near = swap(near, 1)
    far[0], *far[early:] = lax.optimization_barrier((far[0], *far[early:]))
    far[early:] = [swap(rows, 2 + n) for n, rows in enumerate(far[early:])]
    chosen = [jnp.concatenate([expert_ids.T.astype(jnp.float32), gate_weights.T], axis=0)]
    while len(chosen) < groups:
        sent = jnp.concatenate(chosen, axis=0)
        got = swap(sent, len(chosen) * NODE_SIZE)
        chosen += jnp.split(got, len(chosen), axis=0)
    weight = proj_weight.T
    summed = residual
    begin = 0
    after = ()
    paired = columns % LANES == 0 and tensors == 2
    for n, stage in enumerate(stages):
        height = len(stage) * capacity
        if n < early:
            rows = [far[n], swap(far[n][height:], 1)]
        else:
            rows = far[early:]
        parts = combine(
            [chosen[d] for d in stage],
            [own, near, *rows],
            [begin, begin, 0, 0],
            stage[0],
            capacity,
            after,
        )
        begin += height
        after = parts[:1]
        moved = [swap(part, d * NODE_SIZE) if d else part for d, part in zip(stage, parts)]
        if n < early and len(stages) > 1:
            summed = add(summed, moved)
        else:
            for part in moved:
                summed = summed.astype(jnp.float32) + part.astype(jnp.float32)
    stream = summed.astype(jnp.bfloat16)
    if not paired:
        wide = lax.all_gather(stream, "tensor", axis=1, tiled=True).astype(jnp.float32)
        normed = (wide * norm_gain).astype(jnp.bfloat16)
        added = jnp.dot(normed, proj_weight, preferred_element_type=jnp.float32)
        energy = jnp.sum(wide * wide, axis=1)
        inverse = lax.rsqrt(energy / features + epsilon)
        return (stream, (added * inverse[:, None]).astype(jnp.bfloat16))
    held = fetch(weight, *after)
    stream, held = lax.optimization_barrier((stream, held))
    other = lax.ppermute(stream, "tensor", [(i, i ^ 1) for i in range(tensors)])
    gain = norm_gain.reshape(1, features)
    carried = project(gain, held, stream)
    (latents,) = project(gain, held, other, 1, carried, features)
    return (stream, latents)


def solution(mesh):
    return jax.shard_map(
        on_device,
        mesh=mesh,
        in_specs=(
            P("expert", None, None),
            P("expert", None, "tensor"),
            P("expert", None),
            P("expert", None),
            P("expert", "tensor"),
            P(),
            P(None, "tensor"),
        ),
        out_specs=(P("expert", "tensor"), P("expert", "tensor")),
        check_vma=False,
    )
```
